32 devices in a mesh: dp: 8 (over z, x), pipe: 4 (over y, core).
Axes of the slice: x: 2, y: 2, z: 4, core: 2. Of those that a mesh axis runs over, the one named last changes fastest.
Arguments:
- tokens: bfloat16 [64, 64, 3072], P('dp'), may hold values from -40 to 40
- segments: int32 [64, 64], P('dp'), may hold values from 0 to 5, never falling along the last dimension, each value on 1 to 24 neighbouring positions
- keep_mask: int32 [64, 64], P('dp'), may hold values 0 or 1
- norm_gain: float32 [4, 3072], P('pipe'), may hold values from 0.5 to 2
- norm_bias: float32 [4, 3072], P('pipe'), may hold values from -3 to 3
- w_qkv: bfloat16 [4, 3072, 4608], P('pipe', 'dp'), may hold values from -0.109375 to 0.109375
- w_out: bfloat16 [4, 1536, 3072], P('pipe', 'dp'), may hold values from -0.15625 to 0.15625
Outputs:
- layer_outputs: bfloat16 [4, 64, 64, 3072], P('pipe', 'dp')
The draws below stay inside these ranges and needn't reach their ends.
Inputs may be any that keep to these rules, and one draw needn't show every extreme that they name: `segments`: image numbers never fall along a sequence; every image spans 1 to 24 patches and one spans exactly 24.
All inputs are finite; a program needn't handle non-finite values. No bound on the sum of `keep_mask` on one device may be relied on, other than what follows from the above.
Results may differ from the reference program's by a relative error of at most 0.013.
Values may be sent and summed in bfloat16 or wider, within the bound.
A program may use at most 128 MiB of HBM per device.

```python
import math
import jax
import jax.numpy as jnp
import numpy as np
from jax import lax

D = 3072
HEADS = 24
HD = 64
GROUPS = 32
IMGS = 6
LEN = 64
INNER = 1536
SEGMOST = 24
SEQS = 64
LAYERS = 4


def draw_tokens(key, part):
    subkeys = jax.random.split(jax.random.fold_in(key, 11), 3)
    base = jnp.clip(jax.random.normal(subkeys[0], (SEQS, LEN, D), jnp.float32), -4.0, 4.0)
    row_scale = jnp.exp(jax.random.uniform(subkeys[1], (SEQS, LEN, 1), jnp.float32, math.log(0.4), math.log(4.0)))
    col_scale = jnp.exp(jax.random.uniform(subkeys[2], (1, 1, D), jnp.float32, math.log(0.5), math.log(2.0)))
    return (base * row_scale * col_scale).astype(jnp.bfloat16)


def place_ends(result, key, smallest, largest):
    shape = result.shape
    index_at = [jax.random.randint(jax.random.fold_in(key, axis), (), 0, shape[axis]) for axis in range(len(shape))]
    result = result.at[tuple(index_at)].set(smallest)
    longest = shape.index(max(shape))
    index_at[longest] = (index_at[longest] + 1) % shape[longest]
    return result.at[tuple(index_at)].set(largest)


def block_levels(key, shape, cuts, smallest, top_value):
    loudness, own = 1.0, jax.random.fold_in(key, 6)
    for axis_at, blocks in cuts:
        steps = jnp.exp(jax.random.uniform(jax.random.fold_in(own, axis_at), (blocks,), jnp.float32, smallest / len(cuts), top_value / len(cuts)))
        loudness = loudness * jnp.repeat(steps, shape[axis_at] // blocks).reshape([-1 if axis == axis_at else 1 for axis in range(len(shape))])
    return loudness


def length_profile(number_of, total, reach, skew):
    loads = [(1 << 20) // math.isqrt(standing ** skew) + 1 for standing in range(2, number_of + 1)]
    rest, given = total - reach - (number_of - 1), [1] * (number_of - 1)
    while rest > 0:
        movable = [i for i in range(number_of - 1) if given[i] < reach]
        mass, budget = sum([loads[i] for i in movable]), rest
        for i in movable:
            addition = min(reach - given[i], max(1, budget * loads[i] // mass), rest)
            given[i] = given[i] + addition
            rest = rest - addition
    return np.array([reach] + given)


def uneven_parts(rng, amount, total, bound, skew):
    if amount == 2:
        one = jax.random.randint(rng, (), max(1, total - bound), min(bound, total - 1) + 1)
        return jnp.stack([one, total - one])
    sizes = jnp.asarray(length_profile(amount, total, bound, skew), jnp.int32)
    couples = (amount - 1) // 2
    donor, taker = sizes[1:1 + 2 * couples:2], sizes[2:2 + 2 * couples:2]
    room = jnp.minimum(donor - 1, bound - taker)
    moved = jax.random.randint(jax.random.fold_in(rng, 1), (couples,), 0, 1 << 20) % (room + 1)
    sizes = sizes.at[1:1 + 2 * couples:2].set(donor - moved).at[2:2 + 2 * couples:2].set(taker + moved)
    return sizes[jax.random.permutation(jax.random.fold_in(rng, 2), amount)]


def scatter_about(own_key, dims, scale, reach, cuts=(), kind=jnp.bfloat16):
    loudness = block_levels(own_key, dims, cuts, -0.22, 0.18) if cuts else 1.0
    result = jax.random.normal(own_key, dims, jnp.float32) * scale * loudness
    return jnp.minimum(jnp.maximum(result, -reach), reach).astype(kind)


def setup_inputs(seed: int = 0) -> dict:
    arg_keys = jax.random.split(jax.random.key(seed), 8)
    return {
        "tokens": draw_tokens(jax.random.fold_in(arg_keys[7], 71), 0),
        "segments": jax.vmap(lambda own: jnp.searchsorted(jnp.cumsum(uneven_parts(own, IMGS, LEN, SEGMOST, 2)), jnp.arange(LEN), side="right"))(jax.random.split(arg_keys[1], SEQS)).reshape((SEQS, LEN)).astype(jnp.int32),
        "keep_mask": place_ends((jax.random.randint(arg_keys[2], (SEQS, LEN), 0, 8) < 7).astype(jnp.int32), jax.random.fold_in(arg_keys[2], 1), 0, 1),
        "norm_gain": jnp.clip(jnp.exp(math.log(2.0) - 1.3862944 * jax.random.uniform(arg_keys[3], (LAYERS, D), jnp.float32) ** block_levels(arg_keys[3], (LAYERS, D), ((0, 4),), -0.2, 0.2)), 0.5, 2.0),
        "norm_bias": scatter_about(arg_keys[4], (LAYERS, D), 0.5, 3.0, ((0, 4),), jnp.float32),
        "w_qkv": scatter_about(arg_keys[5], (LAYERS, D, 3 * INNER), D ** -0.5, 0.109375, ((0, 4), (1, 8))),
        "w_out": scatter_about(arg_keys[6], (LAYERS, INNER, D), INNER ** -0.5, 0.15625, ((0, 4), (1, 8))),
    }


norm_eps = 1e-05

def group_normed(stream, seg_row, keep_row, gain, bias_row):
    length = stream.shape[0]
    group_width = D // GROUPS
    values = stream.astype(jnp.float32).reshape(length, GROUPS, group_width)
    member = ((seg_row[:, None] == jnp.arange(IMGS, dtype=jnp.int32)[None, :]) & (keep_row[:, None] > 0)).astype(jnp.float32)
    counted = jnp.maximum(lax.optimization_barrier(jnp.sum(member, axis=0)) * group_width, 1.0)
    img_sum = jnp.dot(member.T, lax.optimization_barrier(jnp.sum(values, axis=2)), precision=lax.Precision.HIGHEST)
    img_mean = img_sum / counted[:, None]
    tok_mean = jnp.dot(member, img_mean, precision=lax.Precision.HIGHEST)
    centred = values - tok_mean[:, :, None]
    img_var = jnp.dot(member.T, lax.optimization_barrier(jnp.sum(centred * centred, axis=2)), precision=lax.Precision.HIGHEST) / counted[:, None]
    tok_var = jnp.dot(member, img_var, precision=lax.Precision.HIGHEST)
    normed = (centred * lax.rsqrt(tok_var + norm_eps)[:, :, None]).reshape(length, D)
    normed = (normed * gain[None, :] + bias_row[None, :]) * keep_row[:, None].astype(jnp.float32)
    return normed.astype(jnp.bfloat16)

def one_layer(stream, seg_row, keep_row, gain, bias_row, qkv_weight, out_weight):
    length = stream.shape[0]
    normed = group_normed(stream, seg_row, keep_row, gain, bias_row)
    projected = jnp.dot(normed, qkv_weight, preferred_element_type=jnp.float32)
    query_rows = projected[:, :INNER].reshape(length, HEADS, HD)
    key_rows = projected[:, INNER:2 * INNER].reshape(length, HEADS, HD)
    value_rows = projected[:, 2 * INNER:].reshape(length, HEADS, HD).astype(jnp.bfloat16)
    query_rows = (query_rows * lax.rsqrt(lax.optimization_barrier(jnp.mean(query_rows * query_rows, axis=2, keepdims=True)) + 1e-06)).astype(jnp.bfloat16)
    key_rows = (key_rows * lax.rsqrt(lax.optimization_barrier(jnp.mean(key_rows * key_rows, axis=2, keepdims=True)) + 1e-06)).astype(jnp.bfloat16)
    scores = jnp.einsum('qhd,khd->hqk', query_rows.astype(jnp.float32), key_rows.astype(jnp.float32)) / math.sqrt(HD)
    keep_float = keep_row.astype(jnp.float32)
    allowed = (seg_row[:, None] == seg_row[None, :]).astype(jnp.float32) * keep_float[:, None] * keep_float[None, :]
    expo = jnp.exp(scores) * allowed[None, :, :]
    denominator = lax.optimization_barrier(jnp.sum(expo, axis=2)) + (1.0 - keep_float)[None, :]
    probs = (expo / denominator[:, :, None]).astype(jnp.bfloat16)
    attended = jnp.einsum('hqk,khd->qhd', probs.astype(jnp.float32), value_rows.astype(jnp.float32))
    attended = attended.reshape(length, INNER).astype(jnp.bfloat16)
    branch = jnp.dot(attended, out_weight, preferred_element_type=jnp.float32)
    return (stream.astype(jnp.float32) + branch).astype(jnp.bfloat16)

def reference(tokens, segments, keep_mask, norm_gain, norm_bias, w_qkv, w_out):
    stream = tokens
    saved = []
    for layer_no in range(LAYERS):

        def apply_one(stream_row, seg_row, keep_row):
            return one_layer(stream_row, seg_row, keep_row, norm_gain[layer_no], norm_bias[layer_no], w_qkv[layer_no], w_out[layer_no])
        stream = lax.map(lambda packed: apply_one(packed[0], packed[1], packed[2]), (stream, segments, keep_mask))
        saved.append(stream)
    return jnp.stack(saved)
```

```python
import functools
import math

import jax
import jax.numpy as jnp
from jax import lax
from jax.experimental import pallas as pl
from jax.experimental.pallas import tpu as pltpu
from jax.sharding import PartitionSpec as P

HD = 64
GROUPS = 32
LANES = 128
WIDE = 256
PAIR = 2
MESH = pl.DeviceIdType.MESH
norm_eps = 1e-05


def pieces(rows):
    sixth = rows // 6
    return [(0, sixth, True), (sixth, 3 * sixth, False), (4 * sixth, 2 * sixth, False)]


def gather_events(nz, nx):
    events = []
    for dz in range(1 - nz, nz):
        for dx in range(1 - nx, nx):
            for piece in range(3):
                events.append((dz, dx, piece))
    return events


def next_hops(dz, dx, x_first, nz, nx):
    hops = []
    along_z = [1, -1] if dz == 0 else [1 if dz > 0 else -1]
    along_x = [1, -1] if dx == 0 else [1 if dx > 0 else -1]
    if x_first:
        if dz == 0:
            hops += [(0, step) for step in along_x if abs(dx + step) < nx]
        hops += [(step, 0) for step in along_z if abs(dz + step) < nz]
    else:
        if dx == 0:
            hops += [(step, 0) for step in along_z if abs(dz + step) < nz]
        hops += [(0, step) for step in along_x if abs(dx + step) < nx]
    return hops


def gather_kernel(nz, nx, qkv_ref, out_ref, qkv_full, out_full, send_sem, recv_sem, own_sem):
    me = lax.axis_index("dp")
    pipe = lax.axis_index("pipe")
    z = me // nx
    x = me % nx

    def inside(oz, ox):
        conds = []
        if oz > 0:
            conds.append(z + oz < nz)
        if oz < 0:
            conds.append(z + oz >= 0)
        if ox > 0:
            conds.append(x + ox < nx)
        if ox < 0:
            conds.append(x + ox >= 0)
        return functools.reduce(jnp.logical_and, conds) if conds else None

    def guarded(cond, body):
        if cond is None:
            body()
        else:
            pl.when(cond)(body)

    barrier = pltpu.get_barrier_semaphore()
    neighbours = [(1, 0), (-1, 0), (0, 1), (0, -1)]
    for oz, ox in neighbours:

        def greet(oz=oz, ox=ox):
            pl.semaphore_signal(
                barrier, inc=1, device_id=(me + oz * nx + ox, pipe), device_id_type=MESH
            )

        guarded(inside(oz, ox), greet)
    before = (z + nz - 1) // nz + (x + nx - 1) // nx
    after = (2 * nz - 2 - z) // nz + (2 * nx - 2 - x) // nx
    pl.semaphore_wait(barrier, before + after)

    arrays = [(qkv_ref, qkv_full), (out_ref, out_full)]
    events = gather_events(nz, nx)
    number = {event: at for at, event in enumerate(events)}

    def copy_to(event, hop, which):
        dz, dx, piece = event
        oz, ox = hop
        shard, full = arrays[which]
        rows = shard.shape[0]
        start, size, _ = pieces(rows)[piece]
        source = me - dz * nx - dx
        here = pl.ds(pl.multiple_of(source * rows + start, 16), size)
        src = shard.at[pl.ds(start, size)] if (dz, dx) == (0, 0) else full.at[here]
        slot = number[(dz + oz, dx + ox, piece)]
        return pltpu.make_async_remote_copy(
            src_ref=src,
            dst_ref=full.at[here],
            send_sem=send_sem.at[which, slot],
            recv_sem=recv_sem.at[which, slot],
            device_id=(me + oz * nx + ox, pipe),
            device_id_type=MESH,
        )

    def arrival(event, which):
        dz, dx, piece = event
        shard, full = arrays[which]
        rows = shard.shape[0]
        start, size, _ = pieces(rows)[piece]
        here = full.at[pl.ds(pl.multiple_of((me - dz * nx - dx) * rows + start, 16), size)]
        return pltpu.make_async_copy(here, here, recv_sem.at[which, number[event]])

    own = []
    for which, (shard, full) in enumerate(arrays):
        rows = shard.shape[0]
        own.append(
            pltpu.make_async_copy(
                shard, full.at[pl.ds(pl.multiple_of(me * rows, 16), rows)], own_sem.at[which]
            )
        )

    def order(event):
        dz, dx, piece = event
        x_first = pieces(6)[piece][2]
        leaf = not next_hops(dz, dx, x_first, nz, nx)
        return (leaf, abs(dz) + abs(dx), abs(dx) if not x_first else 0, piece)

    for event in sorted(events, key=order):
        dz, dx, piece = event
        hops = next_hops(dz, dx, pieces(6)[piece][2], nz, nx)

        def work(event=event, hops=hops):
            for which in range(2):
                if event[:2] != (0, 0):
                    arrival(event, which).wait()
                for hop in hops:
                    guarded(inside(*hop), lambda: copy_to(event, hop, which).start())

        guarded(inside(-dz, -dx), work)
        if event[:2] == (0, 0) and piece == 2:
            for copy in own:
                copy.start()
    for copy in own:
        copy.wait()
    for event in events:
        dz, dx, piece = event
        hops = next_hops(dz, dx, pieces(6)[piece][2], nz, nx)

        def finish(event=event, hops=hops):
            for which in range(2):
                for hop in hops:
                    guarded(inside(*hop), lambda: copy_to(event, hop, which).wait_send())

        if hops:
            guarded(inside(-dz, -dx), finish)


def gathered(qkv, out, nz, nx):
    slots = len(gather_events(nz, nx))
    count = nz * nx
    return pl.pallas_call(
        functools.partial(gather_kernel, nz, nx),
        out_shape=[
            jax.ShapeDtypeStruct((count * qkv.shape[0], qkv.shape[1]), qkv.dtype),
            jax.ShapeDtypeStruct((count * out.shape[0], out.shape[1]), out.dtype),
        ],
        in_specs=[pl.BlockSpec(memory_space=pl.ANY)] * 2,
        out_specs=[pl.BlockSpec(memory_space=pl.ANY)] * 2,
        scratch_shapes=[
            pltpu.SemaphoreType.DMA((2, slots)),
            pltpu.SemaphoreType.DMA((2, slots)),
            pltpu.SemaphoreType.DMA((2,)),
        ],
        compiler_params=pltpu.CompilerParams(collective_id=0, has_side_effects=True),
        name="gather_weights",
    )(qkv, out)


def split_dot(value, ones, parts):
    total = None
    for _ in range(parts):
        high = value.astype(jnp.bfloat16)
        term = jnp.dot(high, ones, preferred_element_type=jnp.float32)
        total = term if total is None else total + term
        value = value - high.astype(jnp.float32)
    return total


def layer_kernel(
    steps, group_width, x_ref, allowed_ref, keep_ref, gain_ref, bias_ref, group_ref, spread_ref,
    heads_ref, wq_ref, wk_ref, wv_ref, wo_ref, result_ref, normed_ref, total_ref,
):
    step = pl.program_id(0)
    rows = x_ref.shape[0]
    allowed = allowed_ref[...]
    keep = keep_ref[...]

    @pl.when(step == 0)
    def _():
        group = group_ref[...]
        spread = spread_ref[...]
        count = jnp.maximum(jnp.sum(allowed, axis=1, keepdims=True) * group_width, 1.0)
        sums = jnp.dot(x_ref[...], group, preferred_element_type=jnp.float32)
        mean = jnp.dot(
            allowed, sums, precision=lax.Precision.HIGHEST, preferred_element_type=jnp.float32
        ) / count
        centred = x_ref[...].astype(jnp.float32) - split_dot(mean, spread, 3)
        squares = split_dot(centred * centred, group, 2)
        var = jnp.dot(
            allowed, squares, precision=lax.Precision.HIGHEST, preferred_element_type=jnp.float32
        ) / count
        scale = split_dot(lax.rsqrt(var + norm_eps), spread, 3)
        normed = (centred * scale * gain_ref[...] + bias_ref[...]) * keep
        normed_ref[...] = normed.astype(jnp.bfloat16)
        total_ref[...] = x_ref[...].astype(jnp.float32)

    normed = normed_ref[...]
    ones = heads_ref[...]

    def unit(w_ref):
        got = jnp.dot(normed, w_ref[...], preferred_element_type=jnp.float32)
        square = split_dot(got * got, ones, 2) * (1.0 / HD)
        return (got * lax.rsqrt(square + 1e-06)).astype(jnp.bfloat16)

    query = unit(wq_ref)
    key = unit(wk_ref)
    value = jnp.dot(normed, wv_ref[...], preferred_element_type=jnp.float32).astype(jnp.bfloat16)
    lane = lax.broadcasted_iota(jnp.int32, (rows, LANES), 1)
    low = lane < HD
    low_mask = jnp.where(low, 1.0, 0.0).astype(jnp.bfloat16)
    high_mask = jnp.where(low, 0.0, 1.0).astype(jnp.bfloat16)
    allowed_both = jnp.concatenate([allowed, allowed], axis=0)
    spare = 1.0 - jnp.concatenate([keep, keep], axis=0)
    attended = []
    for at in range(0, WIDE, LANES):
        q, k, v = (a[:, at : at + LANES] for a in (query, key, value))
        both = jnp.concatenate([q * low_mask, q * high_mask], axis=0)
        scores = lax.dot_general(
            both, k, (((1,), (1,)), ((), ())), preferred_element_type=jnp.float32
        ) * (1.0 / math.sqrt(HD))
        expo = jnp.exp(scores) * allowed_both
        probs = (expo / (jnp.sum(expo, axis=1, keepdims=True) + spare)).astype(jnp.bfloat16)
        mixed = jnp.dot(probs, v, preferred_element_type=jnp.float32)
        attended.append(jnp.where(low, mixed[:rows], mixed[rows:]).astype(jnp.bfloat16))
    attended = jnp.concatenate(attended, axis=1)
    total_ref[...] += jnp.dot(attended, wo_ref[...], preferred_element_type=jnp.float32)

    @pl.when(step == steps - 1)
    def _():
        result_ref[...] = total_ref[...].astype(jnp.bfloat16)


def layer(stream, allowed, keep, gain, bias, masks, qkv, out):
    rows, width = stream.shape
    inner = out.shape[0]
    steps = inner // WIDE
    group, spread, heads = masks

    def whole(array):
        return pl.BlockSpec(array.shape, lambda j: (0, 0))

    def columns(part):
        return pl.BlockSpec((width, WIDE), lambda j: (0, part * steps + j))

    small = [stream, allowed, keep, gain, bias, group, spread, heads]
    return pl.pallas_call(
        functools.partial(layer_kernel, steps, width // GROUPS),
        grid=(steps,),
        out_shape=jax.ShapeDtypeStruct((rows, width), jnp.bfloat16),
        in_specs=[whole(a) for a in small]
        + [columns(0), columns(1), columns(2), pl.BlockSpec((WIDE, width), lambda j: (j, 0))],
        out_specs=pl.BlockSpec((rows, width), lambda j: (0, 0)),
        scratch_shapes=[
            pltpu.VMEM((rows, width), jnp.bfloat16),
            pltpu.VMEM((rows, width), jnp.float32),
        ],
        compiler_params=pltpu.CompilerParams(vmem_limit_bytes=48 * 1024 * 1024),
        cost_estimate=pl.CostEstimate(
            flops=8 * rows * width * inner, bytes_accessed=8 * width * inner, transcendentals=0
        ),
        name="layer",
    )(*small, qkv, qkv, qkv, out)


def local(nz, nx, tokens, segments, keep_mask, norm_gain, norm_bias, w_qkv, w_out):
    section = lax.axis_index("pipe")
    sections = lax.axis_size("pipe")
    seqs, length, width = tokens.shape
    rows = PAIR * length
    micro = seqs // PAIR
    qkv, out = gathered(w_qkv[0], w_out[0], nz, nx)

    group = (
        jnp.arange(width)[:, None] // (width // GROUPS) == jnp.arange(LANES)[None, :]
    ).astype(jnp.bfloat16)
    heads = (
        jnp.arange(WIDE)[:, None] // HD == jnp.arange(WIDE)[None, :] // HD
    ).astype(jnp.bfloat16)
    masks = (group, group.T, heads)

    kept = keep_mask.reshape(micro, rows) > 0
    images = segments.reshape(micro, rows)
    place = jnp.arange(rows) // length
    allowed = (
        (images[:, :, None] == images[:, None, :])
        & (place[:, None] == place[None, :])[None]
        & kept[:, :, None]
        & kept[:, None, :]
    ).astype(jnp.float32)
    keep = kept.astype(jnp.float32)[:, :, None]
    flat = tokens.reshape(micro, rows, width)

    incoming = jnp.zeros((rows, width), jnp.bfloat16)
    results = []
    ticks = micro + sections - 1
    for tick in range(ticks):
        index = jnp.clip(tick - section, 0, micro - 1)
        stream = jnp.where(section == 0, flat[min(tick, micro - 1)], incoming)
        result = layer(
            stream,
            lax.dynamic_index_in_dim(allowed, index, 0, keepdims=False),
            lax.dynamic_index_in_dim(keep, index, 0, keepdims=False),
            norm_gain,
            norm_bias,
            masks,
            qkv,
            out,
        )
        results.append(result)
        if tick < ticks - 1:
            incoming = lax.ppermute(
                result, "pipe", [(source, source + 1) for source in range(sections - 1)]
            )
    stacked = jnp.stack(results)
    mine = lax.dynamic_slice_in_dim(stacked, section, micro, 0)
    return mine.reshape(1, seqs, length, width)


def solution(mesh):
    placed = (
        P("dp", None, None),
        P("dp", None),
        P("dp", None),
        P("pipe", None),
        P("pipe", None),
        P("pipe", "dp", None),
        P("pipe", "dp", None),
    )
    nx = max(1, mesh.shape["pipe"] // 2)
    while mesh.shape["dp"] % nx:
        nx -= 1
    nz = mesh.shape["dp"] // nx
    return jax.shard_map(
        functools.partial(local, nz, nx),
        mesh=mesh,
        in_specs=placed,
        out_specs=P("pipe", "dp", None, None),
        check_vma=False,
    )
```
